128 devices in a mesh: replica: 16 (over y_hi, x, core), fsdp: 8 (over y_lo, z).
Axes of the slice: x: 4, y: 4 (y_hi: 2, y_lo: 2; y = y_hi * 2 + y_lo), z: 4, core: 2. Of those that a mesh axis runs over, the one named last changes fastest.
Arguments:
- acts: bfloat16 [16384, 12288], P(('replica', 'fsdp')), may hold values from -15 to 15
- cotangent: bfloat16 [16384, 1024], P(('replica', 'fsdp')), may hold values from -7 to 7
- weights: bfloat16 [16, 12288, 1024], P('replica', 'fsdp'), may hold values from -0.03125 to 0.03125, as said below
- base: float32 [12288, 128], P('fsdp'), may hold values from -0.03125 to 0.03125, as said below
- momentum: float32 [12288, 128], P('fsdp'), may hold values from -0.15625 to 0.15625
- exponents: int32 [12288, 1], P('fsdp'), may hold values from 6 to 9
- fragment: int32 [1], replicated, may hold values from 0 to 7
Outputs:
- new_weights: bfloat16 [16, 12288, 1024], P('replica', 'fsdp')
- input_grads: bfloat16 [16384, 12288], P(('replica', 'fsdp'))
- new_base: float32 [12288, 128], P('fsdp')
- new_momentum: float32 [12288, 128], P('fsdp')
The draws below stay inside these ranges and needn't reach their ends.
Inputs may be any that keep to these rules, and one draw needn't show every extreme that they name: `weights`: every entry's magnitude lies between 2 ** -9 and 2 ** -5. `base`: every entry's magnitude lies between 2 ** -9 and 2 ** -5.
All inputs are finite; a program needn't handle non-finite values.
Results may differ from the reference program's by a relative error of at most 0.001.
Values may be sent and summed in bfloat16 or wider, within the bound.
No kernel may reach another device: no remote copies, remote signals or barrier semaphores. Data moves between devices by JAX's collectives and lax.ppermute only.
A program may use at most 128 MiB of HBM per device.

```python
import math
import jax
import jax.numpy as jnp
from jax import lax

D = 12288
V = 1024
FRAGS = 8
BLK = 128
REPLICAS = 16
FC = 128
REP_TOK = 1024
TOKENS = 16384
N_REPLICA = 16


def draw_acts(key, part):
    key = jax.random.fold_in(key, 11)
    first, second = jax.random.split(key)
    values = jax.random.truncated_normal(first, -4.0, 4.0, (TOKENS, D), jnp.float32)
    columns = jnp.arange(D, dtype=jnp.float32) / D
    jitter = jax.random.uniform(second, (D,), jnp.float32, -0.3, 0.3)
    return (values * jnp.exp2(1.6 * columns + jitter)[None, :]).astype(jnp.bfloat16)


def draw_cotangent(key, part):
    key = jax.random.fold_in(key, 12)
    first, second, third = jax.random.split(key, 3)
    values = jax.random.truncated_normal(first, -4.0, 4.0, (TOKENS, V), jnp.float32)
    order = jax.random.permutation(second, REPLICAS).astype(jnp.float32)
    jitter = jax.random.uniform(third, (REPLICAS,), jnp.float32, -0.1, 0.1)
    levels = -2.5 + 3.0 * order / (REPLICAS - 1) + jitter
    scales = jnp.repeat(jnp.exp2(levels), TOKENS // REPLICAS)
    return (values * scales[:, None]).astype(jnp.bfloat16)


def draw_weights(key, part):
    key = jax.random.fold_in(key, 13)
    first, second = jax.random.split(key)
    shape = (REPLICAS, D, V)
    size = jnp.exp2(jax.random.uniform(first, shape, jnp.float32, -2.0, 2.0))
    sign = (2 * jax.random.randint(second, shape, 0, 2) - 1).astype(jnp.float32)
    return (sign * size / 128.0).astype(jnp.bfloat16)


def draw_base(key, part):
    key = jax.random.fold_in(key, 14)
    first, second = jax.random.split(key)
    shape = (D, V // FRAGS)
    size = jnp.exp2(jax.random.uniform(first, shape, jnp.float32, -2.0, 2.0))
    sign = (2 * jax.random.randint(second, shape, 0, 2) - 1).astype(jnp.float32)
    return sign * size / 128.0


def set_ends(array, key, smallest, top_value):
    place = [jax.random.randint(jax.random.fold_in(key, axis), (), 0, length) for axis, length in enumerate(array.shape)]
    main_axis = array.shape.index(max(array.shape))
    neighbour = place[:main_axis] + [(place[main_axis] + 1) % array.shape[main_axis]] + place[main_axis + 1:]
    return array.at[tuple(place)].set(smallest).at[tuple(neighbour)].set(top_value)


def level_of(own_key, extent, cuts, least, top_value):
    level = 1.0
    for dim, parts in cuts:
        draws = jax.random.uniform(jax.random.fold_in(jax.random.fold_in(own_key, 6), dim), (parts,), jnp.float32, least / len(cuts), top_value / len(cuts))
        level = level * jnp.repeat(jnp.exp(draws), extent[dim] // parts).reshape((-1,) + (1,) * (len(extent) - 1 - dim))
    return level


def noise(own_key, extent, width, limit, cuts=(), held_as=jnp.bfloat16):
    drawn = width * jax.random.normal(own_key, extent, jnp.float32)
    if cuts:
        drawn = drawn * level_of(own_key, extent, cuts, -0.22, 0.18)
    return jnp.clip(drawn, -limit, limit).astype(held_as)


def setup_inputs(seed: int = 0) -> dict:
    arg_keys = jax.random.split(jax.random.key(seed), 8)
    return {
        "acts": draw_acts(jax.random.fold_in(arg_keys[7], 71), 0),
        "cotangent": draw_cotangent(jax.random.fold_in(arg_keys[7], 71), 0),
        "weights": draw_weights(jax.random.fold_in(arg_keys[7], 71), 0),
        "base": draw_base(jax.random.fold_in(arg_keys[7], 71), 0),
        "momentum": noise(arg_keys[4], (D, FC), 0.01, 0.15625, ((0, 8),), jnp.float32),
        "exponents": set_ends(jax.random.randint(arg_keys[5], (D, FC // BLK), 6, 10), jax.random.fold_in(arg_keys[5], 1), 6, 9).astype(jnp.int32),
        "fragment": jax.random.randint(arg_keys[6], (1,), 0, FRAGS).astype(jnp.int32),
    }


inner_rate = 8.0
level_cap = 7.0
nesterov_mu = 0.9
outer_rate = 0.7
merge_share = 0.5

def reference(acts, cotangent, weights, base, momentum, exponents, fragment):
    start = (fragment[0] * FC).astype(jnp.int32)
    powers = jnp.exp2(jnp.repeat(exponents.astype(jnp.float32), BLK, axis=1))

    def add_codes(total, shard):
        piece = lax.dynamic_slice_in_dim(shard, start, FC, 1).astype(jnp.float32)
        levels = jnp.floor((base - piece) * powers + 0.5)
        coded = jnp.clip(levels, -level_cap, level_cap).astype(jnp.bfloat16)
        return (total + coded.astype(jnp.float32), None)
    total, unused = lax.scan(add_codes, jnp.zeros((D, FC), jnp.float32), weights)
    decoded = total / powers / N_REPLICA
    new_momentum = nesterov_mu * momentum + decoded
    new_base = base - outer_rate * (decoded + nesterov_mu * new_momentum)
    acts_rep = acts.reshape(N_REPLICA, REP_TOK, D)
    cot_rep = cotangent.reshape(N_REPLICA, REP_TOK, V)
    threshold = math.sqrt(D * V * REP_TOK)

    def inner(items):
        shard, rows, cot_rows = items
        weight_grad = lax.dot_general(rows, cot_rows, (((0,), (0,)), ((), ())), preferred_element_type=jnp.float32)
        grad_norm = jnp.sqrt(jnp.sum(weight_grad * weight_grad))
        factor = 1.0 / jnp.maximum(grad_norm, threshold)
        local = shard.astype(jnp.float32) - inner_rate * factor * weight_grad
        merged = merge_share * new_base + (1.0 - merge_share) * lax.dynamic_slice_in_dim(local, start, FC, 1)
        updated = lax.dynamic_update_slice_in_dim(local.astype(jnp.bfloat16), merged.astype(jnp.bfloat16), start, 1)
        in_grad = lax.dot_general(cot_rows, shard, (((1,), (1,)), ((), ())), preferred_element_type=jnp.float32)
        return (updated, in_grad.astype(jnp.bfloat16))
    new_weights, in_grads = lax.map(inner, (weights, acts_rep, cot_rep))
    return (new_weights, in_grads.reshape(TOKENS, D), new_base, new_momentum)
```

```python
import functools
import math

import jax
import jax.numpy as jnp
from jax import lax
from jax.experimental import pallas as pl
from jax.experimental.pallas import tpu as pltpu
from jax.sharding import PartitionSpec as P

inner_rate = 8.0
level_cap = 7.0
nesterov_mu = 0.9
outer_rate = 0.7
merge_share = 0.5

NY, NZ = 2, 4
N = NY * NZ
N_REPLICA = 16
VMEM = 60 * 1024 * 1024

OFFSETS = ((0, 1), (0, 3), (0, 2), (1, 0), (1, 1), (1, 3), (1, 2))


def shifted(s, offset, sign):
    return ((s // NZ + sign * offset[0]) % NY) * NZ + (s % NZ + sign * offset[1]) % NZ


def shift(x, offset, sign=1):
    return lax.ppermute(x, "fsdp", [(s, shifted(s, offset, sign)) for s in range(N)])


def after(x, *others):
    return lax.optimization_barrier((x, *others))[0]


def pack_kernel(acts, out, held, in_sem, out_sem):
    width = out.shape[2]
    fetches = [
        pltpu.make_async_copy(acts.at[:, pl.ds(k * width, width)], held.at[k], in_sem.at[k]) for k in range(N)
    ]
    stores = [pltpu.make_async_copy(held.at[k], out.at[k], out_sem.at[k]) for k in range(N)]
    for fetch in fetches:
        fetch.start()
    for fetch, store in zip(fetches, stores):
        fetch.wait()
        store.start()
    for store in stores:
        store.wait()


def pack(acts):
    rows, total = acts.shape
    width = total // N
    return pl.pallas_call(
        pack_kernel,
        in_specs=[pl.BlockSpec(memory_space=pl.ANY)],
        out_specs=pl.BlockSpec(memory_space=pl.ANY),
        out_shape=jax.ShapeDtypeStruct((N, rows, width), acts.dtype),
        scratch_shapes=[
            pltpu.VMEM((N, rows, width), acts.dtype),
            pltpu.SemaphoreType.DMA((N,)),
            pltpu.SemaphoreType.DMA((N,)),
        ],
        compiler_params=pltpu.CompilerParams(vmem_limit_bytes=VMEM),
        cost_estimate=pl.CostEstimate(flops=0, transcendentals=0, bytes_accessed=4 * rows * total),
        name="pack",
    )(acts)


TILES = 6
EARLY_FLOPS = 100 * 10**9
LATE_FLOPS = 6 * 10**9


def dx_kernel(n, *refs):
    cots, w, outs = refs[:n], refs[n], refs[n + 1 : 2 * n + 1]
    cot_v, w_v, out_v, cot_sem, w_sem, out_sem = refs[2 * n + 1 :]
    rows = cots[0].shape[0]
    tile = w.shape[0] // TILES
    cot_in = [pltpu.make_async_copy(cots[k], cot_v.at[pl.ds(k * rows, rows)], cot_sem.at[k]) for k in range(n)]
    w_in = [
        pltpu.make_async_copy(w.at[pl.ds(i * tile, tile)], w_v.at[pl.ds(i * tile, tile)], w_sem.at[i])
        for i in range(TILES)
    ]
    for copy in cot_in + w_in:
        copy.start()
    for copy in cot_in:
        copy.wait()
    stores = []
    half = TILES // 2
    for i in range(TILES):
        w_in[i].wait()
        tall = lax.dot_general(
            cot_v[...], w_v[i * tile : (i + 1) * tile], (((1,), (1,)), ((), ())), preferred_element_type=jnp.float32
        )
        for k in range(n):
            out_v[k, :, i * tile : (i + 1) * tile] = tall[k * rows : (k + 1) * rows].astype(out_v.dtype)
        if (i + 1) % half == 0:
            cols = pl.ds((i + 1 - half) * tile, half * tile)
            for k in range(n):
                store = pltpu.make_async_copy(out_v.at[k, :, cols], outs[k].at[:, cols], out_sem.at[len(stores)])
                store.start()
                stores.append(store)
    for store in stores:
        store.wait()


def dx_blocks(cots, w, flops):
    n = len(cots)
    rows, v = cots[0].shape
    width = w.shape[0]
    return pl.pallas_call(
        functools.partial(dx_kernel, n),
        out_shape=[jax.ShapeDtypeStruct((rows, width), w.dtype)] * n,
        in_specs=[pl.BlockSpec(memory_space=pl.ANY)] * (n + 1),
        out_specs=[pl.BlockSpec(memory_space=pl.ANY)] * n,
        scratch_shapes=[
            pltpu.VMEM((n * rows, v), w.dtype),
            pltpu.VMEM((width, v), w.dtype),
            pltpu.VMEM((n, rows, width), w.dtype),
            pltpu.SemaphoreType.DMA((n,)),
            pltpu.SemaphoreType.DMA((TILES,)),
            pltpu.SemaphoreType.DMA((2 * n,)),
        ],
        compiler_params=pltpu.CompilerParams(vmem_limit_bytes=VMEM),
        cost_estimate=pl.CostEstimate(
            flops=flops, transcendentals=0, bytes_accessed=2 * (width * v + n * rows * (v + width))
        ),
        name="dx",
    )(*cots, w)


def wgrad_kernel(src, acts, *refs):
    cots, (out, squares) = refs[:N], refs[N : N + 2]
    acts_v, cot_v, grad_v, acts_sem, cot_sem, out_sem = refs[N + 2 :]
    rows, v = cots[0].shape
    tile = acts.shape[2] // TILES
    cot_in = [
        pltpu.make_async_copy(cots[k], cot_v.at[pl.ds(pl.multiple_of(src[k] * rows, rows), rows)], cot_sem.at[k])
        for k in range(N)
    ]
    acts_in = [
        pltpu.make_async_copy(
            acts.at[:, :, pl.ds(i * tile, tile)], acts_v.at[:, :, pl.ds(i * tile, tile)], acts_sem.at[i]
        )
        for i in range(TILES)
    ]
    for copy in cot_in + acts_in:
        copy.start()
    for copy in cot_in:
        copy.wait()
    total = jnp.zeros((8, 128), jnp.float32)
    stores = []
    for i in range(TILES):
        acts_in[i].wait()
        a = acts_v[:, :, i * tile : (i + 1) * tile].reshape(N * rows, tile)
        grad = lax.dot_general(a, cot_v[...], (((0,), (0,)), ((), ())), preferred_element_type=jnp.float32)
        grad_v[i * tile : (i + 1) * tile] = grad
        part = jnp.sum((grad * grad).reshape(-1, 8, v), axis=0)
        for j in range(0, v, 128):
            total += part[:, j : j + 128]
        store = pltpu.make_async_copy(
            grad_v.at[pl.ds(i * tile, tile)], out.at[pl.ds(i * tile, tile)], out_sem.at[i]
        )
        store.start()
        stores.append(store)
    squares[...] = total
    for store in stores:
        store.wait()


def wgrad(src, acts, cots):
    rows, v = cots[0].shape
    width = acts.shape[2]
    return pl.pallas_call(
        wgrad_kernel,
        in_specs=[pl.BlockSpec(memory_space=pltpu.SMEM)] + [pl.BlockSpec(memory_space=pl.ANY)] * (N + 1),
        out_specs=[pl.BlockSpec(memory_space=pl.ANY), pl.BlockSpec(memory_space=pltpu.VMEM)],
        out_shape=[jax.ShapeDtypeStruct((width, v), jnp.float32), jax.ShapeDtypeStruct((8, 128), jnp.float32)],
        scratch_shapes=[
            pltpu.VMEM(acts.shape, acts.dtype),
            pltpu.VMEM((N * rows, v), acts.dtype),
            pltpu.VMEM((width, v), jnp.float32),
            pltpu.SemaphoreType.DMA((TILES,)),
            pltpu.SemaphoreType.DMA((N,)),
            pltpu.SemaphoreType.DMA((TILES,)),
        ],
        compiler_params=pltpu.CompilerParams(vmem_limit_bytes=VMEM),
        cost_estimate=pl.CostEstimate(
            flops=2 * N * rows * width * v,
            transcendentals=0,
            bytes_accessed=2 * N * rows * (v + width) + 4 * width * v,
        ),
        name="wgrad",
    )(src, acts, *cots)


def update_kernel(scale, start, grad, w, new_base, out, grad_v, w_v, out_v, grad_sem, w_sem, out_sem):
    tile = w.shape[0] // TILES
    spans = [pl.ds(i * tile, tile) for i in range(TILES)]
    loads = []
    for i, rows in enumerate(spans):
        pair = (
            pltpu.make_async_copy(grad.at[rows], grad_v.at[rows], grad_sem.at[i]),
            pltpu.make_async_copy(w.at[rows], w_v.at[rows], w_sem.at[i]),
        )
        for copy in pair:
            copy.start()
        loads.append(pair)
    cols = pl.ds(pl.multiple_of(start[0], 128), new_base.shape[1])
    stores = []
    for i, rows in enumerate(spans):
        for copy in loads[i]:
            copy.wait()
        local = w_v[rows].astype(jnp.float32) - scale[0] * grad_v[rows]
        out_v[rows] = local.astype(out.dtype)
        piece = w_v[rows, cols].astype(jnp.float32) - scale[0] * grad_v[rows, cols]
        merged = merge_share * new_base[rows] + (1.0 - merge_share) * piece
        out_v[rows, cols] = merged.astype(out.dtype)
        store = pltpu.make_async_copy(out_v.at[rows], out.at[rows], out_sem.at[i])
        store.start()
        stores.append(store)
    for store in stores:
        store.wait()


def update(scale, start, grad, w, new_base):
    rows, v = w.shape
    return pl.pallas_call(
        update_kernel,
        out_shape=jax.ShapeDtypeStruct((rows, v), w.dtype),
        in_specs=[pl.BlockSpec(memory_space=pltpu.SMEM)] * 2
        + [pl.BlockSpec(memory_space=pl.ANY)] * 2
        + [pl.BlockSpec(memory_space=pltpu.VMEM)],
        out_specs=pl.BlockSpec(memory_space=pl.ANY),
        scratch_shapes=[
            pltpu.VMEM((rows, v), jnp.float32),
            pltpu.VMEM((rows, v), w.dtype),
            pltpu.VMEM((rows, v), w.dtype),
        ]
        + [pltpu.SemaphoreType.DMA((TILES,))] * 3,
        compiler_params=pltpu.CompilerParams(vmem_limit_bytes=VMEM),
        cost_estimate=pl.CostEstimate(flops=2 * rows * v, transcendentals=0, bytes_accessed=8 * rows * v),
        name="update",
    )(scale, start, grad, w, new_base)


def unpack_kernel(n, width, dst, *refs):
    blocks = refs[:n]
    out, held, in_sem, out_sem = refs[-4:]
    fetches = [pltpu.make_async_copy(blocks[k], held.at[k], in_sem.at[k]) for k in range(n)]
    stores = [
        pltpu.make_async_copy(
            held.at[k], out.at[:, pl.ds(pl.multiple_of(dst[k] * width, width), width)], out_sem.at[k]
        )
        for k in range(n)
    ]
    for fetch in fetches:
        fetch.start()
    for fetch, store in zip(fetches, stores):
        fetch.wait()
        store.start()
    for store in stores:
        store.wait()


def unpack(dst, blocks, prior=None):
    rows, width = blocks[0].shape
    n = len(blocks)
    operands = [dst, *blocks] + ([] if prior is None else [prior])
    return pl.pallas_call(
        functools.partial(unpack_kernel, n, width),
        in_specs=[pl.BlockSpec(memory_space=pltpu.SMEM)]
        + [pl.BlockSpec(memory_space=pl.ANY)] * (len(operands) - 1),
        out_specs=pl.BlockSpec(memory_space=pl.ANY),
        out_shape=jax.ShapeDtypeStruct((rows, N * width), blocks[0].dtype),
        scratch_shapes=[
            pltpu.VMEM((n, rows, width), blocks[0].dtype),
            pltpu.SemaphoreType.DMA((n,)),
            pltpu.SemaphoreType.DMA((n,)),
        ],
        input_output_aliases={} if prior is None else {len(operands) - 1: 0},
        compiler_params=pltpu.CompilerParams(vmem_limit_bytes=VMEM),
        cost_estimate=pl.CostEstimate(flops=0, transcendentals=0, bytes_accessed=4 * n * rows * width),
        name="unpack",
    )(*operands)


GROUPS = [[8 * h + i for i in range(8)] for h in range(2)]


def on_device(acts, cotangent, weights, base, momentum, exponents, fragment):
    shard = weights[0]
    rows, v = cotangent.shape
    width = acts.shape[1] // N
    fc = base.shape[1]
    start = fragment[0] * fc
    me = lax.axis_index("fsdp")
    src = jnp.stack([shifted(me, o, -1) for o in OFFSETS] + [me]).astype(jnp.int32)
    dst = jnp.stack([shifted(me, o, 1) for o in OFFSETS] + [me]).astype(jnp.int32)

    cots = [shift(cotangent, o) for o in OFFSETS[:4]]

    powers = jnp.left_shift(1, exponents).astype(jnp.float32)
    piece = lax.dynamic_slice_in_dim(shard, start, fc, 1).astype(jnp.float32)
    levels = jnp.floor((base - piece) * powers + 0.5)
    codes = jnp.clip(levels, -level_cap, level_cap).astype(jnp.bfloat16)
    parts = codes.reshape(8, width // 8, fc)
    parts = lax.all_to_all(parts, "replica", 0, 0, axis_index_groups=GROUPS, tiled=True)
    part = jnp.sum(parts.astype(jnp.float32), axis=0).astype(jnp.bfloat16)

    packed = after(pack(acts), part)
    columns = lax.all_to_all(packed, "fsdp", 0, 0, tiled=True)

    cots += [shift(cots[3], OFFSETS[0]), shift(cots[3], OFFSETS[1]), shift(cots[2], OFFSETS[3])]

    early = dx_blocks([cotangent] + cots[:4], shard, EARLY_FLOPS)
    late = dx_blocks(cots[4:], shard, LATE_FLOPS)
    own_dx, dx = early[0], [*early[1:], *late]
    back = [shift(d, o, -1) for d, o in zip(dx, OFFSETS)]

    other = lax.ppermute(part, "replica", [(r, (r + 8) % 16) for r in range(16)])
    part = (part.astype(jnp.float32) + other.astype(jnp.float32)).astype(jnp.bfloat16)
    spread = after(jnp.broadcast_to(part[None], (8, *part.shape)), columns)
    total = lax.all_to_all(spread, "replica", 0, 0, axis_index_groups=GROUPS, tiled=True)
    total = total.reshape(width, fc).astype(jnp.float32)
    decoded = total / powers / lax.axis_size("replica")
    new_momentum = nesterov_mu * momentum + decoded
    new_base = base - outer_rate * (decoded + nesterov_mu * new_momentum)

    grad, squares = wgrad(src, columns, cots + [cotangent])
    mine = jnp.broadcast_to(jnp.sum(squares), (N, 8, 128))
    sums = lax.all_to_all(mine, "fsdp", 0, 0, tiled=True)
    norm2 = jnp.sum(sums[:, 0, 0])
    threshold = math.sqrt(N * width * v * N * rows)
    scale = inner_rate / jnp.maximum(jnp.sqrt(norm2), threshold)
    new_w = update(scale[None], start[None], grad, shard, new_base)

    order = jnp.concatenate([dst[N - 1 :], dst[: N - 1]])
    dxs = unpack(order[:6], [own_dx, *back[:5]])
    dxs = unpack(order[6:], back[5:], dxs)
    return new_w[None], dxs, new_base, new_momentum


def solution(mesh):
    return jax.shard_map(
        on_device,
        mesh=mesh,
        in_specs=(
            P(("replica", "fsdp"), None),
            P(("replica", "fsdp"), None),
            P("replica", "fsdp", None),
            P("fsdp", None),
            P("fsdp", None),
            P("fsdp", None),
            P(),
        ),
        out_specs=(
            P("replica", "fsdp", None),
            P(("replica", "fsdp"), None),
            P("fsdp", None),
            P("fsdp", None),
        ),
        check_vma=False,
    )
```

```python
import functools
import math

import jax
import jax.numpy as jnp
from jax import lax
from jax.experimental import pallas as pl
from jax.experimental.pallas import tpu as pltpu
from jax.sharding import PartitionSpec as P

inner_rate = 8.0
level_cap = 7.0
nesterov_mu = 0.9
outer_rate = 0.7
merge_share = 0.5

NY, NZ = 2, 4
N = NY * NZ
N_REPLICA = 16
VMEM = 60 * 1024 * 1024
DX_STRIPS = 3
WGRAD_STRIPS = 2
UPDATE_STRIPS = 4
PACK_FLOPS = 0
DX_FLOPS = 9 * 10**9

OFFSETS = ((0, 1), (0, 3), (0, 2), (1, 0), (1, 1), (1, 3), (1, 2))


def shifted(s, offset, sign):
    return ((s // NZ + sign * offset[0]) % NY) * NZ + (s % NZ + sign * offset[1]) % NZ


def shift(x, offset, sign=1):
    return lax.ppermute(x, "fsdp", [(s, shifted(s, offset, sign)) for s in range(N)])


def after(x, *others):
    return lax.optimization_barrier((x, *others))[0]


def pack_kernel(acts, out, held, in_sem, out_sem):
    width = out.shape[2]
    fetches = [
        pltpu.make_async_copy(acts.at[:, pl.ds(k * width, width)], held.at[k], in_sem.at[k]) for k in range(N)
    ]
    stores = [pltpu.make_async_copy(held.at[k], out.at[k], out_sem.at[k]) for k in range(N)]
    for fetch in fetches:
        fetch.start()
    for fetch, store in zip(fetches, stores):
        fetch.wait()
        store.start()
    for store in stores:
        store.wait()


def pack(acts):
    rows, total = acts.shape
    width = total // N
    return pl.pallas_call(
        pack_kernel,
        in_specs=[pl.BlockSpec(memory_space=pl.ANY)],
        out_specs=pl.BlockSpec(memory_space=pl.ANY),
        out_shape=jax.ShapeDtypeStruct((N, rows, width), acts.dtype),
        scratch_shapes=[
            pltpu.VMEM((N, rows, width), acts.dtype),
            pltpu.SemaphoreType.DMA((N,)),
            pltpu.SemaphoreType.DMA((N,)),
        ],
        compiler_params=pltpu.CompilerParams(vmem_limit_bytes=VMEM),
        cost_estimate=pl.CostEstimate(flops=PACK_FLOPS, transcendentals=0, bytes_accessed=4 * rows * total),
        name="pack",
    )(acts)


def spans(size, parts):
    return [(i * size // parts, size // parts) for i in range(parts)]


def dx_kernel(n, *refs):
    cots, w, outs = refs[:n], refs[n], refs[n + 1 : 2 * n + 1]
    cot_v, w_v, out_v, cot_sem, w_sem, out_sem = refs[2 * n + 1 :]
    rows = cots[0].shape[0]
    strips = spans(w.shape[0], DX_STRIPS)
    cot_in = [pltpu.make_async_copy(cots[k], cot_v.at[pl.ds(k * rows, rows)], cot_sem.at[k]) for k in range(n)]
    w_in = [
        pltpu.make_async_copy(w.at[pl.ds(a, d)], w_v.at[pl.ds(a, d)], w_sem.at[i]) for i, (a, d) in enumerate(strips)
    ]
    for copy in w_in[:1] + cot_in + w_in[1:]:
        copy.start()
    for copy in cot_in:
        copy.wait()
    stores = []
    for i, (a, d) in enumerate(strips):
        w_in[i].wait()
        tall = lax.dot_general(
            cot_v[...], w_v[a : a + d], (((1,), (1,)), ((), ())), preferred_element_type=jnp.float32
        )
        for k in range(n):
            out_v[k, :, a : a + d] = tall[k * rows : (k + 1) * rows].astype(out_v.dtype)
        for k in range(n):
            cols = pl.ds(a, d)
            store = pltpu.make_async_copy(out_v.at[k, :, cols], outs[k].at[:, cols], out_sem.at[len(stores)])
            store.start()
            stores.append(store)
    for store in stores:
        store.wait()


def dx_blocks(cots, w):
    n = len(cots)
    rows, v = cots[0].shape
    width = w.shape[0]
    return pl.pallas_call(
        functools.partial(dx_kernel, n),
        out_shape=[jax.ShapeDtypeStruct((rows, width), w.dtype)] * n,
        in_specs=[pl.BlockSpec(memory_space=pl.ANY)] * (n + 1),
        out_specs=[pl.BlockSpec(memory_space=pl.ANY)] * n,
        scratch_shapes=[
            pltpu.VMEM((n * rows, v), w.dtype),
            pltpu.VMEM((width, v), w.dtype),
            pltpu.VMEM((n, rows, width), w.dtype),
            pltpu.SemaphoreType.DMA((n,)),
            pltpu.SemaphoreType.DMA((DX_STRIPS,)),
            pltpu.SemaphoreType.DMA((DX_STRIPS * n,)),
        ],
        compiler_params=pltpu.CompilerParams(vmem_limit_bytes=VMEM),
        cost_estimate=pl.CostEstimate(
            flops=DX_FLOPS, transcendentals=0, bytes_accessed=2 * (width * v + n * rows * (v + width))
        ),
        name="dx",
    )(*cots, w)


def wgrad_kernel(index, acts, *refs):
    cots, (out, squares) = refs[:N], refs[N : N + 2]
    acts_v, cot_v, grad_v, acts_sem, cot_sem, out_sem = refs[N + 2 :]
    rows, v = cots[0].shape
    strips = spans(acts.shape[2], WGRAD_STRIPS)
    cot_in = [
        pltpu.make_async_copy(cots[k], cot_v.at[pl.ds(pl.multiple_of(index[k] * rows, rows), rows)], cot_sem.at[k])
        for k in range(N)
    ]
    acts_in = [
        pltpu.make_async_copy(acts.at[:, :, pl.ds(a, d)], acts_v.at[:, :, pl.ds(a, d)], acts_sem.at[i])
        for i, (a, d) in enumerate(strips)
    ]
    for copy in acts_in[:1] + cot_in + acts_in[1:]:
        copy.start()
    for copy in cot_in:
        copy.wait()
    total = jnp.zeros((8, 128), jnp.float32)
    stores = []
    for i, (a, d) in enumerate(strips):
        acts_in[i].wait()
        part = acts_v[:, :, a : a + d].reshape(N * rows, d)
        grad = lax.dot_general(part, cot_v[...], (((0,), (0,)), ((), ())), preferred_element_type=jnp.float32)
        grad_v[a : a + d] = grad
        square = jnp.sum((grad * grad).reshape(-1, 8, v), axis=0)
        for j in range(0, v, 128):
            total += square[:, j : j + 128]
        store = pltpu.make_async_copy(grad_v.at[pl.ds(a, d)], out.at[pl.ds(a, d)], out_sem.at[i])
        store.start()
        stores.append(store)
    squares[...] = jnp.full(squares.shape, jnp.sum(total), jnp.float32)
    for store in stores:
        store.wait()


def wgrad(index, acts, cots):
    rows, v = cots[0].shape
    width = acts.shape[2]
    return pl.pallas_call(
        wgrad_kernel,
        in_specs=[pl.BlockSpec(memory_space=pltpu.SMEM)] + [pl.BlockSpec(memory_space=pl.ANY)] * (N + 1),
        out_specs=[pl.BlockSpec(memory_space=pl.ANY), pl.BlockSpec(memory_space=pltpu.VMEM)],
        out_shape=[
            jax.ShapeDtypeStruct((width, v), jnp.float32),
            jax.ShapeDtypeStruct((N, 8, 128), jnp.float32),
        ],
        scratch_shapes=[
            pltpu.VMEM(acts.shape, acts.dtype),
            pltpu.VMEM((N * rows, v), acts.dtype),
            pltpu.VMEM((width, v), jnp.float32),
            pltpu.SemaphoreType.DMA((WGRAD_STRIPS,)),
            pltpu.SemaphoreType.DMA((N,)),
            pltpu.SemaphoreType.DMA((WGRAD_STRIPS,)),
        ],
        compiler_params=pltpu.CompilerParams(vmem_limit_bytes=VMEM),
        cost_estimate=pl.CostEstimate(flops=0, transcendentals=0, bytes_accessed=0),
        name="wgrad",
    )(index, acts, *cots)


def update_kernel(threshold, start, sums, grad, w, new_base, out, grad_v, w_v, base_v, out_v, in_sem, out_sem):
    loads = []
    strips = spans(w.shape[0], UPDATE_STRIPS)
    for i, (a, d) in enumerate(strips):
        rows = pl.ds(a, d)
        pairs = ((grad, grad_v), (w, w_v), (new_base, base_v))
        group = [
            pltpu.make_async_copy(p.at[rows], q.at[rows], in_sem.at[i * len(pairs) + j])
            for j, (p, q) in enumerate(pairs)
        ]
        for copy in group:
            copy.start()
        loads.append(group)
    norm2 = jnp.sum(sums[:, 0, 0:1])
    scale = inner_rate / jnp.maximum(jnp.sqrt(norm2), threshold)
    cols = pl.ds(pl.multiple_of(start[0], 128), base_v.shape[1])
    stores = []
    for i, (a, d) in enumerate(strips):
        rows = pl.ds(a, d)
        for copy in loads[i]:
            copy.wait()
        local = w_v[rows].astype(jnp.float32) - scale * grad_v[rows]
        out_v[rows] = local.astype(out.dtype)
        piece = w_v[rows, cols].astype(jnp.float32) - scale * grad_v[rows, cols]
        merged = merge_share * base_v[rows] + (1.0 - merge_share) * piece
        out_v[rows, cols] = merged.astype(out.dtype)
        store = pltpu.make_async_copy(out_v.at[rows], out.at[rows], out_sem.at[i])
        store.start()
        stores.append(store)
    for store in stores:
        store.wait()


def update(threshold, start, sums, grad, w, new_base):
    rows, v = w.shape
    return pl.pallas_call(
        functools.partial(update_kernel, threshold),
        out_shape=jax.ShapeDtypeStruct((rows, v), w.dtype),
        in_specs=[pl.BlockSpec(memory_space=pltpu.SMEM), pl.BlockSpec(memory_space=pltpu.VMEM)]
        + [pl.BlockSpec(memory_space=pl.ANY)] * 3,
        out_specs=pl.BlockSpec(memory_space=pl.ANY),
        scratch_shapes=[
            pltpu.VMEM((rows, v), jnp.float32),
            pltpu.VMEM((rows, v), w.dtype),
            pltpu.VMEM(new_base.shape, jnp.float32),
            pltpu.VMEM((rows, v), w.dtype),
            pltpu.SemaphoreType.DMA((3 * UPDATE_STRIPS,)),
            pltpu.SemaphoreType.DMA((UPDATE_STRIPS,)),
        ],
        compiler_params=pltpu.CompilerParams(vmem_limit_bytes=VMEM),
        cost_estimate=pl.CostEstimate(flops=0, transcendentals=0, bytes_accessed=0),
        name="update",
    )(start, sums, grad, w, new_base)


def unpack_kernel(n, first, width, index, *refs):
    blocks = refs[:n]
    out, held, in_sem, out_sem = refs[-4:]
    fetches = [pltpu.make_async_copy(blocks[k], held.at[k], in_sem.at[k]) for k in range(n)]
    stores = [
        pltpu.make_async_copy(
            held.at[k],
            out.at[:, pl.ds(pl.multiple_of(index[first + k] * width, width), width)],
            out_sem.at[k],
        )
        for k in range(n)
    ]
    for fetch in fetches:
        fetch.start()
    for fetch, store in zip(fetches, stores):
        fetch.wait()
        store.start()
    for store in stores:
        store.wait()


def unpack(index, first, blocks, prior=None):
    rows, width = blocks[0].shape
    n = len(blocks)
    operands = [index, *blocks] + ([] if prior is None else [prior])
    return pl.pallas_call(
        functools.partial(unpack_kernel, n, first, width),
        in_specs=[pl.BlockSpec(memory_space=pltpu.SMEM)]
        + [pl.BlockSpec(memory_space=pl.ANY)] * (len(operands) - 1),
        out_specs=pl.BlockSpec(memory_space=pl.ANY),
        out_shape=jax.ShapeDtypeStruct((rows, N * width), blocks[0].dtype),
        scratch_shapes=[
            pltpu.VMEM((n, rows, width), blocks[0].dtype),
            pltpu.SemaphoreType.DMA((n,)),
            pltpu.SemaphoreType.DMA((n,)),
        ],
        input_output_aliases={} if prior is None else {len(operands) - 1: 0},
        compiler_params=pltpu.CompilerParams(vmem_limit_bytes=VMEM),
        cost_estimate=pl.CostEstimate(flops=0, transcendentals=0, bytes_accessed=4 * n * rows * width),
        name="unpack",
    )(*operands)


def replica_pairs(kind):
    pairs = []
    for r in range(N_REPLICA):
        up, x, c = r // 8, r // 2 % 4, r % 2
        label = (x + up) % 4
        if kind == "core":
            c ^= 1
        elif kind == "y":
            up ^= 1
        else:
            label ^= kind
        pairs.append((r, up * 8 + (label - up) % 4 * 2 + c))
    return pairs


def trade(x, kind):
    return lax.ppermute(x, "replica", replica_pairs(kind))


def add(*terms):
    return sum(t.astype(jnp.float32) for t in terms).astype(jnp.bfloat16)


def pick(x, place):
    return lax.dynamic_index_in_dim(x, place, 0, False)


def sum_cores(x, core):
    low, high = x[:, 0], x[:, 1]
    return add(jnp.where(core == 0, low, high), trade(jnp.where(core == 0, high, low), "core"))


def sum_labels(x, label):
    return add(pick(x, label), *[trade(pick(x, label ^ d), d) for d in (1, 2, 3)])


def gather_labels(x, label):
    blocks = [x] + [trade(x, d) for d in (1, 2, 3)]
    out = []
    for place in range(4):
        d = label ^ place
        out.append(jnp.where(d < 2, jnp.where(d == 0, *blocks[:2]), jnp.where(d == 2, *blocks[2:])))
    return jnp.stack(out)


def gather_cores(x, core):
    other = trade(x, "core")
    return jnp.where(core == 0, jnp.stack([x, other], 1), jnp.stack([other, x], 1))


def on_device(acts, cotangent, weights, base, momentum, exponents, fragment):
    shard = weights[0]
    rows, v = cotangent.shape
    width = acts.shape[1] // N
    fc = base.shape[1]
    start = fragment[0] * fc
    me = lax.axis_index("fsdp")
    early, late = (4, 5, 6, 0), (1, 3, 2)
    index = jnp.stack(
        [shifted(me, o, -1) for o in OFFSETS]
        + [me, me]
        + [shifted(me, OFFSETS[k], 1) for k in early + late]
    ).astype(jnp.int32)

    cots = [shift(cotangent, o) for o in OFFSETS[:4]]

    powers = jnp.left_shift(1, exponents).astype(jnp.float32)
    piece = lax.dynamic_slice_in_dim(shard, start, fc, 1).astype(jnp.float32)
    levels = jnp.floor((base - piece) * powers + 0.5)
    codes = jnp.clip(levels, -level_cap, level_cap).astype(jnp.bfloat16)

    cots += [shift(cots[3], OFFSETS[0]), shift(cots[3], OFFSETS[1]), shift(cots[2], OFFSETS[3])]
    packed = after(pack(acts), cots[0], cots[1], cots[2], cots[3])
    columns = lax.all_to_all(packed, "fsdp", 0, 0, tiled=True)

    replica = lax.axis_index("replica")
    core, label = replica % 2, (replica // 2 + replica // 8) % 4
    part = after(codes, cots[4], cots[5], cots[6]).reshape(4, 2, width // 8, fc)
    part = sum_cores(part, core)
    part = sum_labels(part, label)
    part = add(part, trade(part, "y"))
    dx = dx_blocks(cots + [after(cotangent, part)], shard)
    back = [shift(dx[k], OFFSETS[k], -1) for k in early]
    part = gather_labels(part, label)
    part = gather_cores(part, core)
    back.append(shift(after(dx[late[0]], columns), OFFSETS[late[0]], -1))
    total = part.reshape(width, fc).astype(jnp.float32)
    decoded = total / powers / lax.axis_size("replica")
    new_momentum = nesterov_mu * momentum + decoded
    new_base = base - outer_rate * (decoded + nesterov_mu * new_momentum)
    grad, squares = wgrad(index, columns, cots + [cotangent])
    back += [shift(after(dx[k], squares), OFFSETS[k], -1) for k in late[1:]]
    sums = lax.all_to_all(after(squares, back[3]), "fsdp", 0, 0, tiled=True)
    threshold = math.sqrt(N * width * v * N * rows)
    new_w = update(threshold, start[None], sums, grad, shard, new_base)

    dxs = unpack(index, N, [dx[N - 1], *back])
    return new_w[None], dxs, new_base, new_momentum


def solution(mesh):
    return jax.shard_map(
        on_device,
        mesh=mesh,
        in_specs=(
            P(("replica", "fsdp"), None),
            P(("replica", "fsdp"), None),
            P("replica", "fsdp", None),
            P("fsdp", None),
            P("fsdp", None),
            P("fsdp", None),
            P(),
        ),
        out_specs=(
            P("replica", "fsdp", None),
            P(("replica", "fsdp"), None),
            P("fsdp", None),
            P("fsdp", None),
        ),
        check_vma=False,
    )
```

```python
import functools
import math

import jax
import jax.numpy as jnp
from jax import lax
from jax.experimental import pallas as pl
from jax.experimental.pallas import tpu as pltpu
from jax.sharding import PartitionSpec as P

inner_rate = 8.0
level_cap = 7.0
nesterov_mu = 0.9
outer_rate = 0.7
merge_share = 0.5

NY, NZ = 2, 4
N = NY * NZ
N_REPLICA = 16
VMEM = 60 * 1024 * 1024
DX_STRIPS = 3
WGRAD_STRIPS = 2
UPDATE_STRIPS = 4
PACK_FLOPS = 0
DX_FLOPS = 90 * 10**8

OFFSETS = ((0, 1), (0, 3), (0, 2), (1, 0), (1, 1), (1, 3), (1, 2))


def shifted(s, offset, sign):
    return ((s // NZ + sign * offset[0]) % NY) * NZ + (s % NZ + sign * offset[1]) % NZ


def shift(x, offset, sign=1):
    return lax.ppermute(x, "fsdp", [(s, shifted(s, offset, sign)) for s in range(N)])


def after(x, *others):
    return lax.optimization_barrier((x, *others))[0]


def pack_kernel(acts, out, held, in_sem, out_sem):
    width = out.shape[2]
    fetches = [
        pltpu.make_async_copy(acts.at[:, pl.ds(k * width, width)], held.at[k], in_sem.at[k]) for k in range(N)
    ]
    stores = [pltpu.make_async_copy(held.at[k], out.at[k], out_sem.at[k]) for k in range(N)]
    for fetch in fetches:
        fetch.start()
    for fetch, store in zip(fetches, stores):
        fetch.wait()
        store.start()
    for store in stores:
        store.wait()


def pack(acts):
    rows, total = acts.shape
    width = total // N
    return pl.pallas_call(
        pack_kernel,
        in_specs=[pl.BlockSpec(memory_space=pl.ANY)],
        out_specs=pl.BlockSpec(memory_space=pl.ANY),
        out_shape=jax.ShapeDtypeStruct((N, rows, width), acts.dtype),
        scratch_shapes=[
            pltpu.VMEM((N, rows, width), acts.dtype),
            pltpu.SemaphoreType.DMA((N,)),
            pltpu.SemaphoreType.DMA((N,)),
        ],
        compiler_params=pltpu.CompilerParams(vmem_limit_bytes=VMEM),
        cost_estimate=pl.CostEstimate(flops=PACK_FLOPS, transcendentals=0, bytes_accessed=4 * rows * total),
        name="pack",
    )(acts)


def spans(size, parts):
    return [(i * size // parts, size // parts) for i in range(parts)]


def dx_kernel(n, *refs):
    cots, w, outs = refs[:n], refs[n], refs[n + 1 : 2 * n + 1]
    cot_v, w_v, out_v, cot_sem, w_sem, out_sem = refs[2 * n + 1 :]
    rows = cots[0].shape[0]
    strips = spans(w.shape[0], DX_STRIPS)
    cot_in = [pltpu.make_async_copy(cots[k], cot_v.at[pl.ds(k * rows, rows)], cot_sem.at[k]) for k in range(n)]
    w_in = [
        pltpu.make_async_copy(w.at[pl.ds(a, d)], w_v.at[pl.ds(a, d)], w_sem.at[i]) for i, (a, d) in enumerate(strips)
    ]
    for copy in w_in[:1] + cot_in + w_in[1:]:
        copy.start()
    for copy in cot_in:
        copy.wait()
    stores = []
    for i, (a, d) in enumerate(strips):
        w_in[i].wait()
        tall = lax.dot_general(
            cot_v[...], w_v[a : a + d], (((1,), (1,)), ((), ())), preferred_element_type=jnp.float32
        )
        for k in range(n):
            out_v[k, :, a : a + d] = tall[k * rows : (k + 1) * rows].astype(out_v.dtype)
        for k in range(n):
            cols = pl.ds(a, d)
            store = pltpu.make_async_copy(out_v.at[k, :, cols], outs[k].at[:, cols], out_sem.at[len(stores)])
            store.start()
            stores.append(store)
    for store in stores:
        store.wait()


def dx_blocks(cots, w):
    n = len(cots)
    rows, v = cots[0].shape
    width = w.shape[0]
    return pl.pallas_call(
        functools.partial(dx_kernel, n),
        out_shape=[jax.ShapeDtypeStruct((rows, width), w.dtype)] * n,
        in_specs=[pl.BlockSpec(memory_space=pl.ANY)] * (n + 1),
        out_specs=[pl.BlockSpec(memory_space=pl.ANY)] * n,
        scratch_shapes=[
            pltpu.VMEM((n * rows, v), w.dtype),
            pltpu.VMEM((width, v), w.dtype),
            pltpu.VMEM((n, rows, width), w.dtype),
            pltpu.SemaphoreType.DMA((n,)),
            pltpu.SemaphoreType.DMA((DX_STRIPS,)),
            pltpu.SemaphoreType.DMA((DX_STRIPS * n,)),
        ],
        compiler_params=pltpu.CompilerParams(vmem_limit_bytes=VMEM),
        cost_estimate=pl.CostEstimate(
            flops=DX_FLOPS, transcendentals=0, bytes_accessed=2 * (width * v + n * rows * (v + width))
        ),
        name="dx",
    )(*cots, w)


def wgrad_kernel(index, acts, *refs):
    cots, (out, squares) = refs[:N], refs[N : N + 2]
    acts_v, cot_v, grad_v, acts_sem, cot_sem, out_sem = refs[N + 2 :]
    rows, v = cots[0].shape
    strips = spans(acts.shape[2], WGRAD_STRIPS)
    cot_in = [
        pltpu.make_async_copy(cots[k], cot_v.at[pl.ds(pl.multiple_of(index[k] * rows, rows), rows)], cot_sem.at[k])
        for k in range(N)
    ]
    acts_in = [
        pltpu.make_async_copy(acts.at[:, :, pl.ds(a, d)], acts_v.at[:, :, pl.ds(a, d)], acts_sem.at[i])
        for i, (a, d) in enumerate(strips)
    ]
    for copy in acts_in[:1] + cot_in + acts_in[1:]:
        copy.start()
    for copy in cot_in:
        copy.wait()
    total = jnp.zeros((8, 128), jnp.float32)
    stores = []
    for i, (a, d) in enumerate(strips):
        acts_in[i].wait()
        part = acts_v[:, :, a : a + d].reshape(N * rows, d)
        grad = lax.dot_general(part, cot_v[...], (((0,), (0,)), ((), ())), preferred_element_type=jnp.float32)
        grad_v[a : a + d] = grad
        square = jnp.sum((grad * grad).reshape(-1, 8, v), axis=0)
        for j in range(0, v, 128):
            total += square[:, j : j + 128]
        store = pltpu.make_async_copy(grad_v.at[pl.ds(a, d)], out.at[pl.ds(a, d)], out_sem.at[i])
        store.start()
        stores.append(store)
    squares[...] = jnp.full(squares.shape, jnp.sum(total), jnp.float32)
    for store in stores:
        store.wait()


def wgrad(index, acts, cots):
    rows, v = cots[0].shape
    width = acts.shape[2]
    return pl.pallas_call(
        wgrad_kernel,
        in_specs=[pl.BlockSpec(memory_space=pltpu.SMEM)] + [pl.BlockSpec(memory_space=pl.ANY)] * (N + 1),
        out_specs=[pl.BlockSpec(memory_space=pl.ANY), pl.BlockSpec(memory_space=pltpu.VMEM)],
        out_shape=[
            jax.ShapeDtypeStruct((width, v), jnp.float32),
            jax.ShapeDtypeStruct((N, 8, 128), jnp.float32),
        ],
        scratch_shapes=[
            pltpu.VMEM(acts.shape, acts.dtype),
            pltpu.VMEM((N * rows, v), acts.dtype),
            pltpu.VMEM((width, v), jnp.float32),
            pltpu.SemaphoreType.DMA((WGRAD_STRIPS,)),
            pltpu.SemaphoreType.DMA((N,)),
            pltpu.SemaphoreType.DMA((WGRAD_STRIPS,)),
        ],
        compiler_params=pltpu.CompilerParams(vmem_limit_bytes=VMEM),
        cost_estimate=pl.CostEstimate(flops=0, transcendentals=0, bytes_accessed=0),
        name="wgrad",
    )(index, acts, *cots)


def update_kernel(threshold, start, sums, grad, w, new_base, out, grad_v, w_v, base_v, out_v, in_sem, out_sem):
    loads = []
    strips = spans(w.shape[0], UPDATE_STRIPS)
    for i, (a, d) in enumerate(strips):
        rows = pl.ds(a, d)
        pairs = ((grad, grad_v), (w, w_v), (new_base, base_v))
        group = [
            pltpu.make_async_copy(p.at[rows], q.at[rows], in_sem.at[i * len(pairs) + j])
            for j, (p, q) in enumerate(pairs)
        ]
        for copy in group:
            copy.start()
        loads.append(group)
    norm2 = jnp.sum(sums[:, 0, 0:1])
    scale = inner_rate / jnp.maximum(jnp.sqrt(norm2), threshold)
    cols = pl.ds(pl.multiple_of(start[0], 128), base_v.shape[1])
    stores = []
    for i, (a, d) in enumerate(strips):
        rows = pl.ds(a, d)
        for copy in loads[i]:
            copy.wait()
        local = w_v[rows].astype(jnp.float32) - scale * grad_v[rows]
        out_v[rows] = local.astype(out.dtype)
        piece = w_v[rows, cols].astype(jnp.float32) - scale * grad_v[rows, cols]
        merged = merge_share * base_v[rows] + (1.0 - merge_share) * piece
        out_v[rows, cols] = merged.astype(out.dtype)
        store = pltpu.make_async_copy(out_v.at[rows], out.at[rows], out_sem.at[i])
        store.start()
        stores.append(store)
    for store in stores:
        store.wait()


def update(threshold, start, sums, grad, w, new_base):
    rows, v = w.shape
    return pl.pallas_call(
        functools.partial(update_kernel, threshold),
        out_shape=jax.ShapeDtypeStruct((rows, v), w.dtype),
        in_specs=[pl.BlockSpec(memory_space=pltpu.SMEM), pl.BlockSpec(memory_space=pltpu.VMEM)]
        + [pl.BlockSpec(memory_space=pl.ANY)] * 3,
        out_specs=pl.BlockSpec(memory_space=pl.ANY),
        scratch_shapes=[
            pltpu.VMEM((rows, v), jnp.float32),
            pltpu.VMEM((rows, v), w.dtype),
            pltpu.VMEM(new_base.shape, jnp.float32),
            pltpu.VMEM((rows, v), w.dtype),
            pltpu.SemaphoreType.DMA((3 * UPDATE_STRIPS,)),
            pltpu.SemaphoreType.DMA((UPDATE_STRIPS,)),
        ],
        compiler_params=pltpu.CompilerParams(vmem_limit_bytes=48 * 1024 * 1024),
        cost_estimate=pl.CostEstimate(flops=0, transcendentals=0, bytes_accessed=0),
        name="update",
    )(start, sums, grad, w, new_base)


def unpack_kernel(n, first, width, index, *refs):
    blocks = refs[:n]
    out, held, in_sem, out_sem = refs[-4:]
    fetches = [pltpu.make_async_copy(blocks[k], held.at[k], in_sem.at[k]) for k in range(n)]
    stores = [
        pltpu.make_async_copy(
            held.at[k],
            out.at[:, pl.ds(pl.multiple_of(index[first + k] * width, width), width)],
            out_sem.at[k],
        )
        for k in range(n)
    ]
    for fetch in fetches:
        fetch.start()
    for fetch, store in zip(fetches, stores):
        fetch.wait()
        store.start()
    for store in stores:
        store.wait()


def unpack(index, first, blocks, prior=None):
    rows, width = blocks[0].shape
    n = len(blocks)
    operands = [index, *blocks] + ([] if prior is None else [prior])
    return pl.pallas_call(
        functools.partial(unpack_kernel, n, first, width),
        in_specs=[pl.BlockSpec(memory_space=pltpu.SMEM)]
        + [pl.BlockSpec(memory_space=pl.ANY)] * (len(operands) - 1),
        out_specs=pl.BlockSpec(memory_space=pl.ANY),
        out_shape=jax.ShapeDtypeStruct((rows, N * width), blocks[0].dtype),
        scratch_shapes=[
            pltpu.VMEM((n, rows, width), blocks[0].dtype),
            pltpu.SemaphoreType.DMA((n,)),
            pltpu.SemaphoreType.DMA((n,)),
        ],
        input_output_aliases={} if prior is None else {len(operands) - 1: 0},
        compiler_params=pltpu.CompilerParams(vmem_limit_bytes=24 * 1024 * 1024),
        cost_estimate=pl.CostEstimate(flops=0, transcendentals=0, bytes_accessed=4 * n * rows * width),
        name="unpack",
    )(*operands)


def replica_pairs(kind):
    pairs = []
    for r in range(N_REPLICA):
        up, x, c = r // 8, r // 2 % 4, r % 2
        label = (x + up) % 4
        if kind == "core":
            c ^= 1
        elif kind == "y":
            up ^= 1
        else:
            label ^= kind
        pairs.append((r, up * 8 + (label - up) % 4 * 2 + c))
    return pairs


def trade(x, kind):
    return lax.ppermute(x, "replica", replica_pairs(kind))


def add(*terms):
    return sum(t.astype(jnp.float32) for t in terms).astype(jnp.bfloat16)


def pick(x, place):
    return lax.dynamic_index_in_dim(x, place, 0, False)


def sum_cores(x, core):
    low, high = x[:, 0], x[:, 1]
    return add(jnp.where(core == 0, low, high), trade(jnp.where(core == 0, high, low), "core"))


def sum_labels(x, label):
    return add(pick(x, label), *[trade(pick(x, label ^ d), d) for d in (1, 2, 3)])


def gather_labels(x, label):
    blocks = [x] + [trade(x, d) for d in (1, 2, 3)]
    out = []
    for place in range(4):
        d = label ^ place
        out.append(jnp.where(d < 2, jnp.where(d == 0, *blocks[:2]), jnp.where(d == 2, *blocks[2:])))
    return jnp.stack(out)


def gather_cores(x, core):
    other = trade(x, "core")
    return jnp.where(core == 0, jnp.concatenate([x, other], 1), jnp.concatenate([other, x], 1))


def on_device(acts, cotangent, weights, base, momentum, exponents, fragment):
    shard = weights[0]
    rows, v = cotangent.shape
    width = acts.shape[1] // N
    fc = base.shape[1]
    start = fragment[0] * fc
    me = lax.axis_index("fsdp")
    early, late = (4, 5, 6, 0, 1), (2, 3)
    index = jnp.stack(
        [shifted(me, o, -1) for o in OFFSETS]
        + [me, me]
        + [shifted(me, OFFSETS[k], 1) for k in early + late]
    ).astype(jnp.int32)

    cots = [shift(cotangent, o) for o in OFFSETS[:4]]

    powers = jnp.left_shift(1, exponents).astype(jnp.float32)
    piece = lax.dynamic_slice_in_dim(shard, start, fc, 1).astype(jnp.float32)
    levels = jnp.floor((base - piece) * powers + 0.5)
    codes = jnp.clip(levels, -level_cap, level_cap).astype(jnp.bfloat16)

    cots += [shift(cots[3], OFFSETS[0]), shift(cots[3], OFFSETS[1]), shift(cots[2], OFFSETS[3])]
    packed = after(pack(acts), cots[0], cots[1], cots[2], cots[3])
    columns = lax.all_to_all(packed, "fsdp", 0, 0, tiled=True)

    replica = lax.axis_index("replica")
    core, label = replica % 2, (replica // 2 + replica // 8) % 4
    part = after(codes, cots[4], cots[5], cots[6]).reshape(4, 2, width // 8, fc)
    part = sum_cores(part, core)
    part = sum_labels(part, label)
    other = trade(part, "y")
    dx = dx_blocks(cots + [after(cotangent, part)], shard)
    part = add(part, after(other, dx[late[0]]))
    back = [shift(dx[k], OFFSETS[k], -1) for k in early]
    part = gather_labels(part, label)
    part = gather_cores(part, core)
    total = part.reshape(width, fc).astype(jnp.float32)
    decoded = total / powers / lax.axis_size("replica")
    new_momentum = nesterov_mu * momentum + decoded
    new_base = base - outer_rate * (decoded + nesterov_mu * new_momentum)
    grad, squares = wgrad(index, columns, cots + [cotangent])
    back.append(shift(after(dx[late[0]], squares), OFFSETS[late[0]], -1))
    back.append(shift(after(dx[late[1]], squares), OFFSETS[late[1]], -1))
    sums = lax.all_to_all(after(squares, back[3], back[4]), "fsdp", 0, 0, tiled=True)
    threshold = math.sqrt(N * width * v * N * rows)
    new_w = update(threshold, start[None], sums, grad, shard, new_base)

    dxs = unpack(index, N, [dx[N - 1], *back])
    return new_w[None], dxs, new_base, new_momentum


def solution(mesh):
    return jax.shard_map(
        on_device,
        mesh=mesh,
        in_specs=(
            P(("replica", "fsdp"), None),
            P(("replica", "fsdp"), None),
            P("replica", "fsdp", None),
            P("fsdp", None),
            P("fsdp", None),
            P("fsdp", None),
            P(),
        ),
        out_specs=(
            P("replica", "fsdp", None),
            P(("replica", "fsdp"), None),
            P("fsdp", None),
            P("fsdp", None),
        ),
        check_vma=False,
    )
```

```python
import functools
import math

import jax
import jax.numpy as jnp
from jax import lax
from jax.experimental import pallas as pl
from jax.experimental.pallas import tpu as pltpu
from jax.sharding import PartitionSpec as P

inner_rate = 8.0
level_cap = 7.0
nesterov_mu = 0.9
outer_rate = 0.7
merge_share = 0.5

NY, NZ = 2, 4
N = NY * NZ
N_REPLICA = 16
VMEM = 60 * 1024 * 1024
DX_STRIPS = 3
WGRAD_STRIPS = 2
UPDATE_STRIPS = 4
PACK_FLOPS = 0
DX_FLOPS = 90 * 10**8

OFFSETS = ((0, 1), (0, 3), (0, 2), (1, 0), (1, 1), (1, 3), (1, 2))


def shifted(s, offset, sign):
    return ((s // NZ + sign * offset[0]) % NY) * NZ + (s % NZ + sign * offset[1]) % NZ


def shift(x, offset, sign=1):
    return lax.ppermute(x, "fsdp", [(s, shifted(s, offset, sign)) for s in range(N)])


def after(x, *others):
    return lax.optimization_barrier((x, *others))[0]


def pack_kernel(acts, out, held, in_sem, out_sem):
    width = out.shape[2]
    fetches = [
        pltpu.make_async_copy(acts.at[:, pl.ds(k * width, width)], held.at[k], in_sem.at[k]) for k in range(N)
    ]
    stores = [pltpu.make_async_copy(held.at[k], out.at[k], out_sem.at[k]) for k in range(N)]
    for fetch in fetches:
        fetch.start()
    for fetch, store in zip(fetches, stores):
        fetch.wait()
        store.start()
    for store in stores:
        store.wait()


def pack(acts):
    rows, total = acts.shape
    width = total // N
    return pl.pallas_call(
        pack_kernel,
        in_specs=[pl.BlockSpec(memory_space=pl.ANY)],
        out_specs=pl.BlockSpec(memory_space=pl.ANY),
        out_shape=jax.ShapeDtypeStruct((N, rows, width), acts.dtype),
        scratch_shapes=[
            pltpu.VMEM((N, rows, width), acts.dtype),
            pltpu.SemaphoreType.DMA((N,)),
            pltpu.SemaphoreType.DMA((N,)),
        ],
        compiler_params=pltpu.CompilerParams(vmem_limit_bytes=VMEM),
        cost_estimate=pl.CostEstimate(flops=PACK_FLOPS, transcendentals=0, bytes_accessed=4 * rows * total),
        name="pack",
    )(acts)


def spans(size, parts):
    return [(i * size // parts, size // parts) for i in range(parts)]


def dx_kernel(n, *refs):
    cots, w, outs = refs[:n], refs[n], refs[n + 1 : 2 * n + 1]
    cot_v, w_v, out_v, cot_sem, w_sem, out_sem = refs[2 * n + 1 :]
    rows = cots[0].shape[0]
    strips = spans(w.shape[0], DX_STRIPS)
    cot_in = [pltpu.make_async_copy(cots[k], cot_v.at[pl.ds(k * rows, rows)], cot_sem.at[k]) for k in range(n)]
    w_in = [
        pltpu.make_async_copy(w.at[pl.ds(a, d)], w_v.at[pl.ds(a, d)], w_sem.at[i]) for i, (a, d) in enumerate(strips)
    ]
    for copy in w_in[:1] + cot_in + w_in[1:]:
        copy.start()
    for copy in cot_in:
        copy.wait()
    stores = []
    for i, (a, d) in enumerate(strips):
        w_in[i].wait()
        tall = lax.dot_general(
            cot_v[...], w_v[a : a + d], (((1,), (1,)), ((), ())), preferred_element_type=jnp.float32
        )
        for k in range(n):
            out_v[k, :, a : a + d] = tall[k * rows : (k + 1) * rows].astype(out_v.dtype)
        for k in range(n):
            cols = pl.ds(a, d)
            store = pltpu.make_async_copy(out_v.at[k, :, cols], outs[k].at[:, cols], out_sem.at[len(stores)])
            store.start()
            stores.append(store)
    for store in stores:
        store.wait()


def dx_blocks(cots, w):
    n = len(cots)
    rows, v = cots[0].shape
    width = w.shape[0]
    return pl.pallas_call(
        functools.partial(dx_kernel, n),
        out_shape=[jax.ShapeDtypeStruct((rows, width), w.dtype)] * n,
        in_specs=[pl.BlockSpec(memory_space=pl.ANY)] * (n + 1),
        out_specs=[pl.BlockSpec(memory_space=pl.ANY)] * n,
        scratch_shapes=[
            pltpu.VMEM((n * rows, v), w.dtype),
            pltpu.VMEM((width, v), w.dtype),
            pltpu.VMEM((n, rows, width), w.dtype),
            pltpu.SemaphoreType.DMA((n,)),
            pltpu.SemaphoreType.DMA((DX_STRIPS,)),
            pltpu.SemaphoreType.DMA((DX_STRIPS * n,)),
        ],
        compiler_params=pltpu.CompilerParams(vmem_limit_bytes=VMEM),
        cost_estimate=pl.CostEstimate(
            flops=DX_FLOPS, transcendentals=0, bytes_accessed=2 * (width * v + n * rows * (v + width))
        ),
        name="dx",
    )(*cots, w)


def wgrad_kernel(index, acts, *refs):
    cots, (out, squares) = refs[:N], refs[N : N + 2]
    acts_v, cot_v, grad_v, acts_sem, cot_sem, out_sem = refs[N + 2 :]
    rows, v = cots[0].shape
    strips = spans(acts.shape[2], WGRAD_STRIPS)
    cot_in = [
        pltpu.make_async_copy(cots[k], cot_v.at[pl.ds(pl.multiple_of(index[k] * rows, rows), rows)], cot_sem.at[k])
        for k in range(N)
    ]
    acts_in = [
        pltpu.make_async_copy(acts.at[:, :, pl.ds(a, d)], acts_v.at[:, :, pl.ds(a, d)], acts_sem.at[i])
        for i, (a, d) in enumerate(strips)
    ]
    for copy in acts_in[:1] + cot_in + acts_in[1:]:
        copy.start()
    for copy in cot_in:
        copy.wait()
    total = jnp.zeros((8, 128), jnp.float32)
    stores = []
    for i, (a, d) in enumerate(strips):
        acts_in[i].wait()
        part = acts_v[:, :, a : a + d].reshape(N * rows, d)
        grad = lax.dot_general(part, cot_v[...], (((0,), (0,)), ((), ())), preferred_element_type=jnp.float32)
        grad_v[a : a + d] = grad
        square = jnp.sum((grad * grad).reshape(-1, 8, v), axis=0)
        for j in range(0, v, 128):
            total += square[:, j : j + 128]
        store = pltpu.make_async_copy(grad_v.at[pl.ds(a, d)], out.at[pl.ds(a, d)], out_sem.at[i])
        store.start()
        stores.append(store)
    squares[...] = jnp.full(squares.shape, jnp.sum(total), jnp.float32)
    for store in stores:
        store.wait()


def wgrad(index, acts, cots):
    rows, v = cots[0].shape
    width = acts.shape[2]
    return pl.pallas_call(
        wgrad_kernel,
        in_specs=[pl.BlockSpec(memory_space=pltpu.SMEM)] + [pl.BlockSpec(memory_space=pl.ANY)] * (N + 1),
        out_specs=[pl.BlockSpec(memory_space=pl.ANY), pl.BlockSpec(memory_space=pltpu.VMEM)],
        out_shape=[
            jax.ShapeDtypeStruct((width, v), jnp.float32),
            jax.ShapeDtypeStruct((N, 8, 128), jnp.float32),
        ],
        scratch_shapes=[
            pltpu.VMEM(acts.shape, acts.dtype),
            pltpu.VMEM((N * rows, v), acts.dtype),
            pltpu.VMEM((width, v), jnp.float32),
            pltpu.SemaphoreType.DMA((WGRAD_STRIPS,)),
            pltpu.SemaphoreType.DMA((N,)),
            pltpu.SemaphoreType.DMA((WGRAD_STRIPS,)),
        ],
        compiler_params=pltpu.CompilerParams(vmem_limit_bytes=VMEM),
        cost_estimate=pl.CostEstimate(flops=0, transcendentals=0, bytes_accessed=0),
        name="wgrad",
    )(index, acts, *cots)


def update_kernel(threshold, start, sums, grad, w, new_base, out, grad_v, w_v, base_v, out_v, in_sem, out_sem):
    loads = []
    strips = spans(w.shape[0], UPDATE_STRIPS)
    for i, (a, d) in enumerate(strips):
        rows = pl.ds(a, d)
        pairs = ((grad, grad_v), (w, w_v), (new_base, base_v))
        group = [
            pltpu.make_async_copy(p.at[rows], q.at[rows], in_sem.at[i * len(pairs) + j])
            for j, (p, q) in enumerate(pairs)
        ]
        for copy in group:
            copy.start()
        loads.append(group)
    norm2 = jnp.sum(sums[:, 0, 0:1])
    scale = inner_rate / jnp.maximum(jnp.sqrt(norm2), threshold)
    cols = pl.ds(pl.multiple_of(start[0], 128), base_v.shape[1])
    stores = []
    for i, (a, d) in enumerate(strips):
        rows = pl.ds(a, d)
        for copy in loads[i]:
            copy.wait()
        local = w_v[rows].astype(jnp.float32) - scale * grad_v[rows]
        out_v[rows] = local.astype(out.dtype)
        piece = w_v[rows, cols].astype(jnp.float32) - scale * grad_v[rows, cols]
        merged = merge_share * base_v[rows] + (1.0 - merge_share) * piece
        out_v[rows, cols] = merged.astype(out.dtype)
        store = pltpu.make_async_copy(out_v.at[rows], out.at[rows], out_sem.at[i])
        store.start()
        stores.append(store)
    for store in stores:
        store.wait()


def update(threshold, start, sums, grad, w, new_base):
    rows, v = w.shape
    return pl.pallas_call(
        functools.partial(update_kernel, threshold),
        out_shape=jax.ShapeDtypeStruct((rows, v), w.dtype),
        in_specs=[pl.BlockSpec(memory_space=pltpu.SMEM), pl.BlockSpec(memory_space=pltpu.VMEM)]
        + [pl.BlockSpec(memory_space=pl.ANY)] * 3,
        out_specs=pl.BlockSpec(memory_space=pl.ANY),
        scratch_shapes=[
            pltpu.VMEM((rows, v), jnp.float32),
            pltpu.VMEM((rows, v), w.dtype),
            pltpu.VMEM(new_base.shape, jnp.float32),
            pltpu.VMEM((rows, v), w.dtype),
            pltpu.SemaphoreType.DMA((3 * UPDATE_STRIPS,)),
            pltpu.SemaphoreType.DMA((UPDATE_STRIPS,)),
        ],
        compiler_params=pltpu.CompilerParams(vmem_limit_bytes=48 * 1024 * 1024),
        cost_estimate=pl.CostEstimate(flops=0, transcendentals=0, bytes_accessed=0),
        name="update",
    )(start, sums, grad, w, new_base)


def unpack_kernel(n, first, width, index, *refs):
    blocks = refs[:n]
    out, held, in_sem, out_sem = refs[-4:]
    fetches = [pltpu.make_async_copy(blocks[k], held.at[k], in_sem.at[k]) for k in range(n)]
    stores = [
        pltpu.make_async_copy(
            held.at[k],
            out.at[:, pl.ds(pl.multiple_of(index[first + k] * width, width), width)],
            out_sem.at[k],
        )
        for k in range(n)
    ]
    for fetch in fetches:
        fetch.start()
    for fetch, store in zip(fetches, stores):
        fetch.wait()
        store.start()
    for store in stores:
        store.wait()


def unpack(index, first, blocks, prior=None):
    rows, width = blocks[0].shape
    n = len(blocks)
    operands = [index, *blocks] + ([] if prior is None else [prior])
    return pl.pallas_call(
        functools.partial(unpack_kernel, n, first, width),
        in_specs=[pl.BlockSpec(memory_space=pltpu.SMEM)]
        + [pl.BlockSpec(memory_space=pl.ANY)] * (len(operands) - 1),
        out_specs=pl.BlockSpec(memory_space=pl.ANY),
        out_shape=jax.ShapeDtypeStruct((rows, N * width), blocks[0].dtype),
        scratch_shapes=[
            pltpu.VMEM((n, rows, width), blocks[0].dtype),
            pltpu.SemaphoreType.DMA((n,)),
            pltpu.SemaphoreType.DMA((n,)),
        ],
        input_output_aliases={} if prior is None else {len(operands) - 1: 0},
        compiler_params=pltpu.CompilerParams(vmem_limit_bytes=24 * 1024 * 1024),
        cost_estimate=pl.CostEstimate(flops=0, transcendentals=0, bytes_accessed=4 * n * rows * width),
        name="unpack",
    )(*operands)


def replica_pairs(kind):
    pairs = []
    for r in range(N_REPLICA):
        up, x, c = r // 8, r // 2 % 4, r % 2
        label = (x + up) % 4
        if kind == "core":
            c ^= 1
        elif kind == "y":
            up ^= 1
        else:
            label ^= kind
        pairs.append((r, up * 8 + (label - up) % 4 * 2 + c))
    return pairs


def trade(x, kind):
    return lax.ppermute(x, "replica", replica_pairs(kind))


def add(*terms):
    return sum(t.astype(jnp.float32) for t in terms).astype(jnp.bfloat16)


def pick(x, place):
    return lax.dynamic_index_in_dim(x, place, 0, False)


def sum_cores(x, core):
    low, high = x[:, 0], x[:, 1]
    return add(jnp.where(core == 0, low, high), trade(jnp.where(core == 0, high, low), "core"))


def sum_labels(x, label):
    return add(pick(x, label), *[trade(pick(x, label ^ d), d) for d in (1, 2, 3)])


def gather_labels(x, label):
    blocks = [x] + [trade(x, d) for d in (1, 2, 3)]
    out = []
    for place in range(4):
        d = label ^ place
        out.append(jnp.where(d < 2, jnp.where(d == 0, *blocks[:2]), jnp.where(d == 2, *blocks[2:])))
    return jnp.stack(out)


def gather_cores(x, core):
    other = trade(x, "core")
    return jnp.where(core == 0, jnp.concatenate([x, other], 1), jnp.concatenate([other, x], 1))


def on_device(acts, cotangent, weights, base, momentum, exponents, fragment):
    shard = weights[0]
    rows, v = cotangent.shape
    width = acts.shape[1] // N
    fc = base.shape[1]
    start = fragment[0] * fc
    me = lax.axis_index("fsdp")
    early, late = (4, 5, 0, 1), (6, 3, 2)
    index = jnp.stack(
        [shifted(me, o, -1) for o in OFFSETS]
        + [me, me]
        + [shifted(me, OFFSETS[k], 1) for k in early + late]
    ).astype(jnp.int32)

    cots = [shift(cotangent, o) for o in OFFSETS[:4]]

    powers = jnp.left_shift(1, exponents).astype(jnp.float32)
    piece = lax.dynamic_slice_in_dim(shard, start, fc, 1).astype(jnp.float32)
    levels = jnp.floor((base - piece) * powers + 0.5)
    codes = jnp.clip(levels, -level_cap, level_cap).astype(jnp.bfloat16)

    cots += [shift(cots[3], OFFSETS[0]), shift(cots[3], OFFSETS[1]), shift(cots[2], OFFSETS[3])]
    packed = after(pack(acts), cots[0], cots[1], cots[2], cots[3])
    columns = lax.all_to_all(packed, "fsdp", 0, 0, tiled=True)

    replica = lax.axis_index("replica")
    core, label = replica % 2, (replica // 2 + replica // 8) % 4
    part = after(codes, cots[4], cots[5], cots[6], index).reshape(4, 2, width // 8, fc)
    part = sum_cores(part, core)
    part = sum_labels(part, label)
    other = trade(part, "y")
    dx = dx_blocks(cots + [after(cotangent, part)], shard)
    part = add(part, after(other, dx[late[0]]))
    back = [shift(dx[k], OFFSETS[k], -1) for k in early]
    part = gather_labels(part, label)
    part = gather_cores(part, core)
    total = part.reshape(width, fc).astype(jnp.float32)
    decoded = total / powers / lax.axis_size("replica")
    new_momentum = nesterov_mu * momentum + decoded
    new_base = base - outer_rate * (decoded + nesterov_mu * new_momentum)
    grad, squares = wgrad(index, columns, cots + [cotangent])
    back.append(shift(after(dx[late[0]], squares), OFFSETS[late[0]], -1))
    back.append(shift(after(dx[late[1]], squares), OFFSETS[late[1]], -1))
    back.append(shift(after(dx[late[2]], squares), OFFSETS[late[2]], -1))
    sums = lax.all_to_all(squares, "fsdp", 0, 0, tiled=True)
    threshold = math.sqrt(N * width * v * N * rows)
    new_w = update(threshold, start[None], sums, grad, shard, new_base)

    dxs = unpack(index, N, [after(dx[N - 1], new_w), *back[:4]])
    dxs = unpack(index, N + 5, back[4:], dxs)
    return new_w[None], dxs, new_base, new_momentum


def solution(mesh):
    return jax.shard_map(
        on_device,
        mesh=mesh,
        in_specs=(
            P(("replica", "fsdp"), None),
            P(("replica", "fsdp"), None),
            P("replica", "fsdp", None),
            P("fsdp", None),
            P("fsdp", None),
            P("fsdp", None),
            P(),
        ),
        out_specs=(
            P("replica", "fsdp", None),
            P(("replica", "fsdp"), None),
            P("fsdp", None),
            P("fsdp", None),
        ),
        check_vma=False,
    )
```

```python
import functools
import math

import jax
import jax.numpy as jnp
from jax import lax
from jax.experimental import pallas as pl
from jax.experimental.pallas import tpu as pltpu
from jax.sharding import PartitionSpec as P

inner_rate = 8.0
level_cap = 7.0
nesterov_mu = 0.9
outer_rate = 0.7
merge_share = 0.5

NY, NZ = 2, 4
N = NY * NZ
N_REPLICA = 16
VMEM = 60 * 1024 * 1024
DX_STRIPS = 3
WGRAD_STRIPS = 2
UPDATE_STRIPS = 4
PACK_FLOPS = 0
DX_FLOPS = 90 * 10**8

OFFSETS = ((0, 1), (0, 3), (0, 2), (1, 0), (1, 1), (1, 3), (1, 2))


def shifted(s, offset, sign):
    return ((s // NZ + sign * offset[0]) % NY) * NZ + (s % NZ + sign * offset[1]) % NZ


def shift(x, offset, sign=1):
    return lax.ppermute(x, "fsdp", [(s, shifted(s, offset, sign)) for s in range(N)])


def after(x, *others):
    return lax.optimization_barrier((x, *others))[0]


def pack_kernel(acts, out, held, in_sem, out_sem):
    width = out.shape[2]
    fetches = [
        pltpu.make_async_copy(acts.at[:, pl.ds(k * width, width)], held.at[k], in_sem.at[k]) for k in range(N)
    ]
    stores = [pltpu.make_async_copy(held.at[k], out.at[k], out_sem.at[k]) for k in range(N)]
    for fetch in fetches:
        fetch.start()
    for fetch, store in zip(fetches, stores):
        fetch.wait()
        store.start()
    for store in stores:
        store.wait()


def pack(acts):
    rows, total = acts.shape
    width = total // N
    return pl.pallas_call(
        pack_kernel,
        in_specs=[pl.BlockSpec(memory_space=pl.ANY)],
        out_specs=pl.BlockSpec(memory_space=pl.ANY),
        out_shape=jax.ShapeDtypeStruct((N, rows, width), acts.dtype),
        scratch_shapes=[
            pltpu.VMEM((N, rows, width), acts.dtype),
            pltpu.SemaphoreType.DMA((N,)),
            pltpu.SemaphoreType.DMA((N,)),
        ],
        compiler_params=pltpu.CompilerParams(vmem_limit_bytes=VMEM),
        cost_estimate=pl.CostEstimate(flops=PACK_FLOPS, transcendentals=0, bytes_accessed=4 * rows * total),
        name="pack",
    )(acts)


def spans(size, parts):
    return [(i * size // parts, size // parts) for i in range(parts)]


def dx_kernel(n, *refs):
    cots, w, outs = refs[:n], refs[n], refs[n + 1 : 2 * n + 1]
    cot_v, w_v, out_v, cot_sem, w_sem, out_sem = refs[2 * n + 1 :]
    rows = cots[0].shape[0]
    strips = spans(w.shape[0], DX_STRIPS)
    cot_in = [pltpu.make_async_copy(cots[k], cot_v.at[pl.ds(k * rows, rows)], cot_sem.at[k]) for k in range(n)]
    w_in = [
        pltpu.make_async_copy(w.at[pl.ds(a, d)], w_v.at[pl.ds(a, d)], w_sem.at[i]) for i, (a, d) in enumerate(strips)
    ]
    for copy in w_in[:1] + cot_in + w_in[1:]:
        copy.start()
    for copy in cot_in:
        copy.wait()
    stores = []
    for i, (a, d) in enumerate(strips):
        w_in[i].wait()
        tall = lax.dot_general(
            cot_v[...], w_v[a : a + d], (((1,), (1,)), ((), ())), preferred_element_type=jnp.float32
        )
        for k in range(n):
            out_v[k, :, a : a + d] = tall[k * rows : (k + 1) * rows].astype(out_v.dtype)
        for k in range(n):
            cols = pl.ds(a, d)
            store = pltpu.make_async_copy(out_v.at[k, :, cols], outs[k].at[:, cols], out_sem.at[len(stores)])
            store.start()
            stores.append(store)
    for store in stores:
        store.wait()


def dx_blocks(cots, w):
    n = len(cots)
    rows, v = cots[0].shape
    width = w.shape[0]
    return pl.pallas_call(
        functools.partial(dx_kernel, n),
        out_shape=[jax.ShapeDtypeStruct((rows, width), w.dtype)] * n,
        in_specs=[pl.BlockSpec(memory_space=pl.ANY)] * (n + 1),
        out_specs=[pl.BlockSpec(memory_space=pl.ANY)] * n,
        scratch_shapes=[
            pltpu.VMEM((n * rows, v), w.dtype),
            pltpu.VMEM((width, v), w.dtype),
            pltpu.VMEM((n, rows, width), w.dtype),
            pltpu.SemaphoreType.DMA((n,)),
            pltpu.SemaphoreType.DMA((DX_STRIPS,)),
            pltpu.SemaphoreType.DMA((DX_STRIPS * n,)),
        ],
        compiler_params=pltpu.CompilerParams(vmem_limit_bytes=VMEM),
        cost_estimate=pl.CostEstimate(
            flops=DX_FLOPS, transcendentals=0, bytes_accessed=2 * (width * v + n * rows * (v + width))
        ),
        name="dx",
    )(*cots, w)


def wgrad_kernel(index, acts, *refs):
    cots, (out, squares) = refs[:N], refs[N : N + 2]
    acts_v, cot_v, grad_v, acts_sem, cot_sem, out_sem = refs[N + 2 :]
    rows, v = cots[0].shape
    strips = spans(acts.shape[2], WGRAD_STRIPS)
    cot_in = [
        pltpu.make_async_copy(cots[k], cot_v.at[pl.ds(pl.multiple_of(index[k] * rows, rows), rows)], cot_sem.at[k])
        for k in range(N)
    ]
    acts_in = [
        pltpu.make_async_copy(acts.at[:, :, pl.ds(a, d)], acts_v.at[:, :, pl.ds(a, d)], acts_sem.at[i])
        for i, (a, d) in enumerate(strips)
    ]
    for copy in acts_in[:1] + cot_in + acts_in[1:]:
        copy.start()
    for copy in cot_in:
        copy.wait()
    total = jnp.zeros((8, 128), jnp.float32)
    stores = []
    pieces = [(i, a, d) for i, (a, d) in enumerate(strips[:-1])]
    last, (a, d) = len(strips) - 1, strips[-1]
    pieces += [(last, a, 2 * d // 3), (None, a + 2 * d // 3, d // 3)]
    for j, (i, a, d) in enumerate(pieces):
        if i is not None:
            acts_in[i].wait()
        part = acts_v[:, :, a : a + d].reshape(N * rows, d)
        grad = lax.dot_general(part, cot_v[...], (((0,), (0,)), ((), ())), preferred_element_type=jnp.float32)
        grad_v[a : a + d] = grad
        store = pltpu.make_async_copy(grad_v.at[pl.ds(a, d)], out.at[pl.ds(a, d)], out_sem.at[j])
        store.start()
        stores.append(store)
        square = jnp.sum((grad * grad).reshape(-1, 8, v), axis=0)
        for c in range(0, v, 128):
            total += square[:, c : c + 128]
    squares[...] = jnp.full(squares.shape, jnp.sum(total), jnp.float32)
    for store in stores:
        store.wait()


def wgrad(index, acts, cots):
    rows, v = cots[0].shape
    width = acts.shape[2]
    return pl.pallas_call(
        wgrad_kernel,
        in_specs=[pl.BlockSpec(memory_space=pltpu.SMEM)] + [pl.BlockSpec(memory_space=pl.ANY)] * (N + 1),
        out_specs=[pl.BlockSpec(memory_space=pl.ANY), pl.BlockSpec(memory_space=pltpu.VMEM)],
        out_shape=[
            jax.ShapeDtypeStruct((width, v), jnp.float32),
            jax.ShapeDtypeStruct((N, 8, 128), jnp.float32),
        ],
        scratch_shapes=[
            pltpu.VMEM(acts.shape, acts.dtype),
            pltpu.VMEM((N * rows, v), acts.dtype),
            pltpu.VMEM((width, v), jnp.float32),
            pltpu.SemaphoreType.DMA((WGRAD_STRIPS,)),
            pltpu.SemaphoreType.DMA((N,)),
            pltpu.SemaphoreType.DMA((WGRAD_STRIPS + 1,)),
        ],
        compiler_params=pltpu.CompilerParams(vmem_limit_bytes=VMEM),
        cost_estimate=pl.CostEstimate(flops=0, transcendentals=0, bytes_accessed=0),
        name="wgrad",
    )(index, acts, *cots)


def update_kernel(threshold, start, sums, grad, w, new_base, out, grad_v, w_v, base_v, out_v, in_sem, out_sem):
    loads = []
    strips = spans(w.shape[0], UPDATE_STRIPS)
    for i, (a, d) in enumerate(strips):
        rows = pl.ds(a, d)
        pairs = ((grad, grad_v), (w, w_v), (new_base, base_v))
        group = [
            pltpu.make_async_copy(p.at[rows], q.at[rows], in_sem.at[i * len(pairs) + j])
            for j, (p, q) in enumerate(pairs)
        ]
        for copy in group:
            copy.start()
        loads.append(group)
    norm2 = jnp.sum(sums[:, 0, 0:1])
    scale = inner_rate / jnp.maximum(jnp.sqrt(norm2), threshold)
    cols = pl.ds(pl.multiple_of(start[0], 128), base_v.shape[1])
    stores = []
    for i, (a, d) in enumerate(strips):
        rows = pl.ds(a, d)
        for copy in loads[i]:
            copy.wait()
        local = w_v[rows].astype(jnp.float32) - scale * grad_v[rows]
        out_v[rows] = local.astype(out.dtype)
        piece = w_v[rows, cols].astype(jnp.float32) - scale * grad_v[rows, cols]
        merged = merge_share * base_v[rows] + (1.0 - merge_share) * piece
        out_v[rows, cols] = merged.astype(out.dtype)
        store = pltpu.make_async_copy(out_v.at[rows], out.at[rows], out_sem.at[i])
        store.start()
        stores.append(store)
    for store in stores:
        store.wait()


def update(threshold, start, sums, grad, w, new_base):
    rows, v = w.shape
    return pl.pallas_call(
        functools.partial(update_kernel, threshold),
        out_shape=jax.ShapeDtypeStruct((rows, v), w.dtype),
        in_specs=[pl.BlockSpec(memory_space=pltpu.SMEM), pl.BlockSpec(memory_space=pltpu.VMEM)]
        + [pl.BlockSpec(memory_space=pl.ANY)] * 3,
        out_specs=pl.BlockSpec(memory_space=pl.ANY),
        scratch_shapes=[
            pltpu.VMEM((rows, v), jnp.float32),
            pltpu.VMEM((rows, v), w.dtype),
            pltpu.VMEM(new_base.shape, jnp.float32),
            pltpu.VMEM((rows, v), w.dtype),
            pltpu.SemaphoreType.DMA((3 * UPDATE_STRIPS,)),
            pltpu.SemaphoreType.DMA((UPDATE_STRIPS,)),
        ],
        compiler_params=pltpu.CompilerParams(vmem_limit_bytes=48 * 1024 * 1024),
        cost_estimate=pl.CostEstimate(flops=0, transcendentals=0, bytes_accessed=0),
        name="update",
    )(start, sums, grad, w, new_base)


def unpack_kernel(n, first, width, index, *refs):
    blocks = refs[:n]
    out, held, in_sem, out_sem = refs[-4:]
    fetches = [pltpu.make_async_copy(blocks[k], held.at[k], in_sem.at[k]) for k in range(n)]
    stores = [
        pltpu.make_async_copy(
            held.at[k],
            out.at[:, pl.ds(pl.multiple_of(index[first + k] * width, width), width)],
            out_sem.at[k],
        )
        for k in range(n)
    ]
    for fetch in fetches:
        fetch.start()
    for fetch, store in zip(fetches, stores):
        fetch.wait()
        store.start()
    for store in stores:
        store.wait()


def unpack(index, first, blocks, prior=None):
    rows, width = blocks[0].shape
    n = len(blocks)
    operands = [index, *blocks] + ([] if prior is None else [prior])
    return pl.pallas_call(
        functools.partial(unpack_kernel, n, first, width),
        in_specs=[pl.BlockSpec(memory_space=pltpu.SMEM)]
        + [pl.BlockSpec(memory_space=pl.ANY)] * (len(operands) - 1),
        out_specs=pl.BlockSpec(memory_space=pl.ANY),
        out_shape=jax.ShapeDtypeStruct((rows, N * width), blocks[0].dtype),
        scratch_shapes=[
            pltpu.VMEM((n, rows, width), blocks[0].dtype),
            pltpu.SemaphoreType.DMA((n,)),
            pltpu.SemaphoreType.DMA((n,)),
        ],
        input_output_aliases={} if prior is None else {len(operands) - 1: 0},
        compiler_params=pltpu.CompilerParams(vmem_limit_bytes=24 * 1024 * 1024),
        cost_estimate=pl.CostEstimate(flops=0, transcendentals=0, bytes_accessed=4 * n * rows * width),
        name="unpack",
    )(*operands)


def replica_pairs(kind):
    pairs = []
    for r in range(N_REPLICA):
        up, x, c = r // 8, r // 2 % 4, r % 2
        label = (x + up) % 4
        if kind == "core":
            c ^= 1
        elif kind == "y":
            up ^= 1
        else:
            label ^= kind
        pairs.append((r, up * 8 + (label - up) % 4 * 2 + c))
    return pairs


def trade(x, kind):
    return lax.ppermute(x, "replica", replica_pairs(kind))


def add(*terms):
    return sum(t.astype(jnp.float32) for t in terms).astype(jnp.bfloat16)


def pick(x, place):
    return lax.dynamic_index_in_dim(x, place, 0, False)


def sum_cores(x, core):
    low, high = x[:, 0], x[:, 1]
    return add(jnp.where(core == 0, low, high), trade(jnp.where(core == 0, high, low), "core"))


def sum_labels(x, label):
    return add(pick(x, label), *[trade(pick(x, label ^ d), d) for d in (1, 2, 3)])


def gather_labels(x, label):
    blocks = [x] + [trade(x, d) for d in (1, 2, 3)]
    out = []
    for place in range(4):
        d = label ^ place
        out.append(jnp.where(d < 2, jnp.where(d == 0, *blocks[:2]), jnp.where(d == 2, *blocks[2:])))
    return jnp.stack(out)


def gather_cores(x, core):
    other = trade(x, "core")
    return jnp.where(core == 0, jnp.concatenate([x, other], 1), jnp.concatenate([other, x], 1))


def on_device(acts, cotangent, weights, base, momentum, exponents, fragment):
    shard = weights[0]
    rows, v = cotangent.shape
    width = acts.shape[1] // N
    fc = base.shape[1]
    start = fragment[0] * fc
    me = lax.axis_index("fsdp")
    early, late = (4, 5, 0, 1), (6, 3, 2)
    index = jnp.stack(
        [shifted(me, o, -1) for o in OFFSETS]
        + [me, me]
        + [shifted(me, OFFSETS[k], 1) for k in early + late]
    ).astype(jnp.int32)

    cots = [shift(cotangent, o) for o in OFFSETS[:4]]

    powers = jnp.left_shift(1, exponents).astype(jnp.float32)
    piece = lax.dynamic_slice_in_dim(shard, start, fc, 1).astype(jnp.float32)
    levels = jnp.floor((base - piece) * powers + 0.5)
    codes = jnp.clip(levels, -level_cap, level_cap).astype(jnp.bfloat16)

    cots += [shift(cots[3], OFFSETS[0]), shift(cots[3], OFFSETS[1]), shift(cots[2], OFFSETS[3])]
    packed = after(pack(acts), cots[0], cots[1], cots[2], cots[3])
    columns = lax.all_to_all(packed, "fsdp", 0, 0, tiled=True)

    replica = lax.axis_index("replica")
    core, label = replica % 2, (replica // 2 + replica // 8) % 4
    part = after(codes, cots[4], cots[5], cots[6], index).reshape(4, 2, width // 8, fc)
    part = sum_cores(part, core)
    part = sum_labels(part, label)
    other = trade(part, "y")
    dx = dx_blocks(cots + [after(cotangent, part)], shard)
    part = add(part, after(other, dx[late[0]]))
    back = [shift(dx[k], OFFSETS[k], -1) for k in early]
    part = gather_labels(part, label)
    part = gather_cores(part, core)
    total = part.reshape(width, fc).astype(jnp.float32)
    decoded = total / powers / lax.axis_size("replica")
    new_momentum = nesterov_mu * momentum + decoded
    new_base = base - outer_rate * (decoded + nesterov_mu * new_momentum)
    grad, squares = wgrad(index, columns, cots + [cotangent])
    back.append(shift(after(dx[late[0]], squares), OFFSETS[late[0]], -1))
    back.append(shift(after(dx[late[1]], squares), OFFSETS[late[1]], -1))
    back.append(shift(after(dx[late[2]], squares), OFFSETS[late[2]], -1))
    sums = lax.all_to_all(squares, "fsdp", 0, 0, tiled=True)
    threshold = math.sqrt(N * width * v * N * rows)
    new_w = update(threshold, start[None], sums, grad, shard, new_base)

    dxs = unpack(index, N, [after(dx[N - 1], new_w), *back[:4]])
    dxs = unpack(index, N + 5, back[4:], dxs)
    return new_w[None], dxs, new_base, new_momentum


def solution(mesh):
    return jax.shard_map(
        on_device,
        mesh=mesh,
        in_specs=(
            P(("replica", "fsdp"), None),
            P(("replica", "fsdp"), None),
            P("replica", "fsdp", None),
            P("fsdp", None),
            P("fsdp", None),
            P("fsdp", None),
            P(),
        ),
        out_specs=(
            P("replica", "fsdp", None),
            P(("replica", "fsdp"), None),
            P("fsdp", None),
            P("fsdp", None),
        ),
        check_vma=False,
    )
```
